256 devices in a mesh: wide: 32 (over y_lo, z, core), narrow: 8 (over y_hi, x).
Axes of the slice: x: 4, y: 4 (y_hi: 2, y_lo: 2; y = y_hi * 2 + y_lo), z: 8, core: 2. Of those that a mesh axis runs over, the one named last changes fastest.
Arguments:
- velocity: float32 [3, 256, 256, 512], P(None, 'narrow', 'wide'), may hold values from -6 to 6
- slope_x: float32 [512, 512], replicated, may hold values from -0.25 to 0.25
- curve_x: float32 [512, 512], replicated, may hold values from -0.25 to 0.25
- slope_y: float32 [256, 256], replicated, may hold values from -0.375 to 0.375
- curve_y: float32 [256, 256], replicated, may hold values from -0.375 to 0.375
- slope_z: float32 [256, 256], replicated, may hold values from -0.375 to 0.375
- curve_z: float32 [256, 256], replicated, may hold values from -0.375 to 0.375
Outputs:
- forcing: float32 [3, 256, 256, 512], P(None, 'narrow', 'wide')
The draws below stay inside these ranges and needn't reach their ends.
All inputs are finite; a program needn't handle non-finite values.
Results may differ from the reference program's by a relative error of at most 0.0001.
Values sent between devices are 32-bit elements; how exact they have to be, the bound alone decides.
A program may use at most 128 MiB of HBM per device.

```python
import jax
import jax.numpy as jnp
from jax import lax

NX = 512
NY = 256
NZ = 256


def block_scale(rng, extent, cuts, low, largest):
    def one(dim, blocks):
        draws = jax.random.uniform(jax.random.fold_in(jax.random.fold_in(rng, 6), dim), (blocks,), jnp.float32, low / len(cuts), largest / len(cuts))
        return jnp.repeat(jnp.exp(draws), extent[dim] // blocks).reshape((-1,) + (1,) * (len(extent) - dim - 1))

    level = one(*cuts[0])
    for cut in cuts[1:]:
        level = level * one(*cut)
    return level


def noise(key, dims, deviation, most, shards=(), kind=jnp.bfloat16):
    result = jax.random.normal(key, dims, jnp.float32) * deviation
    if len(shards) > 0:
        result = block_scale(key, dims, shards, -0.22, 0.18) * result
    return jnp.clip(result, min=-most, max=most).astype(kind)


def setup_inputs(seed: int = 0) -> dict:
    key_of = jax.random.split(jax.random.key(seed), 8)
    return {
        "velocity": noise(key_of[0], (3, NY, NZ, NX), 1.0, 6.0, ((1, 8), (2, 32)), jnp.float32),
        "slope_x": noise(key_of[1], (NX, NX), NX ** -0.5, 0.25, (), jnp.float32),
        "curve_x": noise(key_of[2], (NX, NX), NX ** -0.5, 0.25, (), jnp.float32),
        "slope_y": noise(key_of[3], (NY, NY), NY ** -0.5, 0.375, (), jnp.float32),
        "curve_y": noise(key_of[4], (NY, NY), NY ** -0.5, 0.375, (), jnp.float32),
        "slope_z": noise(key_of[5], (NZ, NZ), NZ ** -0.5, 0.375, (), jnp.float32),
        "curve_z": noise(key_of[6], (NZ, NZ), NZ ** -0.5, 0.375, (), jnp.float32),
    }


viscosity = 0.5


def contribution(fields, products, slopes, curves, direction, formula):
    pair = jnp.concatenate([products, fields], axis=0)
    derived = jnp.einsum(formula, slopes, pair, precision=lax.Precision.HIGHEST)
    second_order = jnp.einsum(formula, curves, fields, precision=lax.Precision.HIGHEST)
    return -0.5 * (derived[:3] + fields[direction] * derived[3:]) + viscosity * second_order


def reference(velocity, slope_x, curve_x, slope_y, curve_y, slope_z, curve_z):
    forcing = jnp.zeros(velocity.shape, jnp.float32)
    plans = [(slope_x, curve_x, "xk,cyzk->cyzx"), (slope_y, curve_y, "yk,ckzx->cyzx"), (slope_z, curve_z, "zk,cykx->cyzx")]
    for direction in range(3):
        slopes, curves, formula = plans[direction]
        forcing = forcing + contribution(velocity, velocity * velocity[direction], slopes, curves, direction, formula)
    return forcing
```

```python
import functools

import jax
import jax.numpy as jnp
from jax import lax
from jax.experimental import pallas as pl
from jax.experimental.pallas import tpu as pltpu
from jax.sharding import PartitionSpec as P

MESH = pl.DeviceIdType.MESH
F32 = jnp.float32
BF16 = jnp.bfloat16
Z_ORDER = (2, 0, 1)
Y_ORDER = (1, 2, 0)
OUT_ORDER = (2, 0, 1)


def split(value):
    high = value.astype(BF16)
    return high, (value - high.astype(F32)).astype(BF16)


def product(left, right):
    dot = functools.partial(jnp.dot, preferred_element_type=F32)
    return dot(left[0], right[0]) + (dot(left[0], right[1]) + dot(left[1], right[0]))


def product_t(left, right):
    dot = functools.partial(lax.dot_general, dimension_numbers=(((1,), (1,)), ((), ())), preferred_element_type=F32)
    return dot(left[0], right[0]) + (dot(left[0], right[1]) + dot(left[1], right[0]))


def kernel(
    wide_size, narrow_size,
    vel, sx, cx, sy, cy, sz, cz,
    out,
    velv, opx, opyz, hx, lx, hyz, lyz,
    ysrc, zin, yin, zres, yres, zret, yret, acc,
    load_sem, send_sem, zin_sem, yin_sem, zret_sem, yret_sem, out_sem,
):
    wide = lax.axis_index("wide")
    narrow = lax.axis_index("narrow")
    rows, cols, width = velv.shape[1], velv.shape[2], velv.shape[3]

    load_vel = pltpu.make_async_copy(vel, velv, load_sem.at[0])
    load_vel.start()
    loads = [
        pltpu.make_async_copy(source, target, load_sem.at[1 + k])
        for k, (source, target) in enumerate(
            [(sx, opx.at[0]), (cx, opx.at[1]), (sy, opyz.at[0]), (cy, opyz.at[1]), (sz, opyz.at[2]), (cz, opyz.at[3])]
        )
    ]
    for load in loads:
        load.start()

    barrier = pltpu.get_barrier_semaphore()

    def greet_wide(k, carry):
        pl.semaphore_signal(barrier, inc=1, device_id={"wide": (wide + k) % wide_size}, device_id_type=MESH)
        return carry

    def greet_narrow(k, carry):
        pl.semaphore_signal(barrier, inc=1, device_id={"narrow": (narrow + k) % narrow_size}, device_id_type=MESH)
        return carry

    lax.fori_loop(1, wide_size, greet_wide, 0)
    lax.fori_loop(1, narrow_size, greet_narrow, 0)
    pl.semaphore_wait(barrier, wide_size + narrow_size - 2)

    z_rows = pl.ds(pl.multiple_of(wide * cols, cols), cols)
    y_rows = pl.ds(pl.multiple_of(narrow * rows, rows), rows)

    def send_z(c):
        def one(k, carry):
            to = (wide + k) % wide_size
            pltpu.make_async_remote_copy(
                vel.at[c, to], zin.at[c, z_rows], send_sem.at[0], zin_sem.at[c],
                device_id={"wide": to}, device_id_type=MESH,
            ).start()
            return carry

        lax.fori_loop(1, wide_size, one, 0)

    def send_y(c):
        def one(k, carry):
            to = (narrow + k) % narrow_size
            pltpu.make_async_remote_copy(
                ysrc.at[c, to], yin.at[c, y_rows], send_sem.at[1], yin_sem.at[c],
                device_id={"narrow": to}, device_id_type=MESH,
            ).start()
            return carry

        lax.fori_loop(1, narrow_size, one, 0)

    def return_z(c):
        def one(k, carry):
            to = (wide + k) % wide_size
            pltpu.make_async_remote_copy(
                zres.at[c, pl.ds(pl.multiple_of(to * cols, cols), cols)], zret.at[c, wide], send_sem.at[2], zret_sem.at[c],
                device_id={"wide": to}, device_id_type=MESH,
            ).start()
            return carry

        lax.fori_loop(1, wide_size, one, 0)

    def return_y(c):
        def one(k, carry):
            to = (narrow + k) % narrow_size
            pltpu.make_async_remote_copy(
                yres.at[c, pl.ds(pl.multiple_of(to * rows, rows), rows)], yret.at[c, narrow], send_sem.at[3], yret_sem.at[c],
                device_id={"narrow": to}, device_id_type=MESH,
            ).start()
            return carry

        lax.fori_loop(1, narrow_size, one, 0)

    def lines_up(c):
        for n in range(narrow_size):
            ysrc[c, n] = velv[c, :, n, :]
        yin[c, y_rows] = ysrc[c, narrow]
        zin[c, z_rows] = velv[c, wide]

    send_z(Z_ORDER[0])
    load_vel.wait()
    lines_up(Y_ORDER[0])
    send_y(Y_ORDER[0])
    send_z(Z_ORDER[1])
    lines_up(Y_ORDER[1])
    send_y(Y_ORDER[1])
    send_z(Z_ORDER[2])
    lines_up(Y_ORDER[2])
    send_y(Y_ORDER[2])

    for load in loads:
        load.wait()
    for k in range(2):
        hx[k], lx[k] = split((-0.5, 0.5)[k] * opx[k])
    for k in range(4):
        hyz[k], lyz[k] = split((-0.5, 0.5)[k % 2] * opyz[k])

    def x_part(c, carry):
        along = velv[0].reshape(rows * cols, width)
        field = velv[c].reshape(rows * cols, width)
        pair = split(field)
        total = product_t(split(field * along), (hx[0], lx[0])) + product_t(pair, (hx[1], lx[1]))
        total = total + along * product_t(pair, (hx[0], lx[0]))
        acc[c] = total.reshape(rows, cols, width)
        return carry

    lax.fori_loop(0, 3, x_part, 0)

    def line_part(source, result, operators, direction, c):
        slope, curve = (hyz[operators], lyz[operators]), (hyz[operators + 1], lyz[operators + 1])
        along, field = source[direction], source[c]
        pair = split(field)
        total = product(slope, split(field * along)) + product(curve, pair)
        result[c] = total + along * product(slope, pair)

    def arrived(sem, buffer, blocks, size):
        part = buffer.at[pl.ds(0, (blocks - 1) * size)]
        pltpu.make_async_copy(part, part, sem).wait()

    for step in range(3):
        c = Z_ORDER[step]
        arrived(zin_sem.at[c], zin.at[c], wide_size, cols)
        line_part(zin, zres, 2, 2, c)
        return_z(c)
        zret[c, wide] = zres[c, z_rows]
        c = Y_ORDER[step]
        arrived(yin_sem.at[c], yin.at[c], narrow_size, rows)
        line_part(yin, yres, 0, 1, c)
        return_y(c)
        yret[c, narrow] = yres[c, y_rows]

    writes = []
    for c in OUT_ORDER:
        arrived(zret_sem.at[c], zret.at[c], wide_size, 1)
        acc[c] = acc[c] + zret[c]
        arrived(yret_sem.at[c], yret.at[c], narrow_size, 1)
        for n in range(narrow_size):
            acc[c, :, n, :] = acc[c, :, n, :] + yret[c, n]
        write = pltpu.make_async_copy(acc.at[c], out.at[c], out_sem.at[c])
        write.start()
        writes.append(write)

    for sem, buffer, blocks, size in (
        (send_sem.at[0], zin, wide_size, cols),
        (send_sem.at[1], yin, narrow_size, rows),
        (send_sem.at[2], zin, wide_size, cols),
        (send_sem.at[3], yin, narrow_size, rows),
    ):
        part = buffer.at[:, pl.ds(0, (blocks - 1) * size)]
        pltpu.make_async_copy(part, part, sem).wait()
    for write in writes:
        write.wait()


def on_device(wide_size, narrow_size, velocity, slope_x, curve_x, slope_y, curve_y, slope_z, curve_z):
    _, rows, cols, width = velocity.shape
    z_lines, y_lines = wide_size * cols, narrow_size * rows
    dma = pltpu.SemaphoreType.DMA
    return pl.pallas_call(
        functools.partial(kernel, wide_size, narrow_size),
        out_shape=jax.ShapeDtypeStruct(velocity.shape, F32),
        in_specs=[pl.BlockSpec(memory_space=pl.ANY)] * 7,
        out_specs=pl.BlockSpec(memory_space=pl.ANY),
        scratch_shapes=[
            pltpu.VMEM(velocity.shape, F32),
            pltpu.VMEM((2, width, width), F32),
            pltpu.VMEM((4, z_lines, z_lines), F32),
            pltpu.VMEM((2, width, width), BF16),
            pltpu.VMEM((2, width, width), BF16),
            pltpu.VMEM((4, z_lines, z_lines), BF16),
            pltpu.VMEM((4, z_lines, z_lines), BF16),
            pltpu.VMEM((3, cols, rows, width), F32),
            pltpu.VMEM((3, z_lines, width), F32),
            pltpu.VMEM((3, y_lines, width), F32),
            pltpu.VMEM((3, z_lines, width), F32),
            pltpu.VMEM((3, y_lines, width), F32),
            pltpu.VMEM(velocity.shape, F32),
            pltpu.VMEM((3, cols, rows, width), F32),
            pltpu.VMEM(velocity.shape, F32),
            dma((7,)),
            dma((4,)),
            dma((3,)),
            dma((3,)),
            dma((3,)),
            dma((3,)),
            dma((3,)),
        ],
        compiler_params=pltpu.CompilerParams(
            collective_id=0, has_side_effects=True, vmem_limit_bytes=48 * 1024 * 1024
        ),
    )(velocity, slope_x, curve_x, slope_y, curve_y, slope_z, curve_z)


def solution(mesh):
    return jax.shard_map(
        functools.partial(on_device, mesh.shape["wide"], mesh.shape["narrow"]),
        mesh=mesh,
        in_specs=(P(None, "narrow", "wide", None), P(), P(), P(), P(), P(), P()),
        out_specs=P(None, "narrow", "wide", None),
        check_vma=False,
    )
```

```python
import functools

import jax
import jax.numpy as jnp
from jax import lax
from jax.experimental import pallas as pl
from jax.experimental.pallas import tpu as pltpu
from jax.sharding import PartitionSpec as P

MESH = pl.DeviceIdType.MESH
F32 = jnp.float32
BF16 = jnp.bfloat16
Z_ORDER = (2, 0, 1)
Y_ORDER = (1, 2, 0)


def split(value):
    high = value.astype(BF16)
    return high, (value - high.astype(F32)).astype(BF16)


def product(left, right):
    dot = functools.partial(jnp.dot, preferred_element_type=F32)
    return dot(left[0], right[0]) + (dot(left[0], right[1]) + dot(left[1], right[0]))


def product_t(left, right):
    dot = functools.partial(lax.dot_general, dimension_numbers=(((1,), (1,)), ((), ())), preferred_element_type=F32)
    return dot(left[0], right[0]) + (dot(left[0], right[1]) + dot(left[1], right[0]))


def kernel(
    wide_size, narrow_size,
    vel, sx, cx, sy, cy, sz, cz,
    acc,
    velv, opx, opyz, hx, lx, hyz, lyz,
    ysrc, zin, yin, zres, yres, yret, zret,
    load_sem, send_sem, zin_sem, yin_sem, zret_sem, yret_sem,
):
    wide = lax.axis_index("wide")
    narrow = lax.axis_index("narrow")
    rows, cols, width = velv.shape[1], velv.shape[2], velv.shape[3]

    load_vel = pltpu.make_async_copy(vel, velv, load_sem.at[0])
    load_vel.start()
    loads = [
        pltpu.make_async_copy(source, target, load_sem.at[1 + k])
        for k, (source, target) in enumerate(
            [(sx, opx.at[0]), (cx, opx.at[1]), (sy, opyz.at[0]), (cy, opyz.at[1]), (sz, opyz.at[2]), (cz, opyz.at[3])]
        )
    ]
    for load in loads:
        load.start()

    barrier = pltpu.get_barrier_semaphore()
    deep = wide_size // 4
    y_lo, z, core = wide // (2 * deep), (wide // 2) % deep, wide % 2

    def wide_peer(k):
        turn = k // 4
        far = (deep // 2 - (turn + 1) // 2) * (1 - 2 * ((turn + 1 + core) % 2))
        other_y, other_core = 1 - (k % 4) // 2, 1 - k % 2
        return ((y_lo + other_y) % 2 * deep + (z + far + deep) % deep) * 2 + (core + other_core) % 2

    def greet_wide(k, carry):
        pl.semaphore_signal(barrier, inc=1, device_id={"wide": wide_peer(k)}, device_id_type=MESH)
        return carry

    def greet_narrow(k, carry):
        pl.semaphore_signal(barrier, inc=1, device_id={"narrow": (narrow + k) % narrow_size}, device_id_type=MESH)
        return carry

    lax.fori_loop(0, wide_size - 1, greet_wide, 0)
    lax.fori_loop(1, narrow_size, greet_narrow, 0)
    pl.semaphore_wait(barrier, wide_size + narrow_size - 2)

    z_rows = pl.ds(pl.multiple_of(wide * cols, cols), cols)
    y_rows = pl.ds(pl.multiple_of(narrow * rows, rows), rows)

    def send_z(c):
        def one(k, carry):
            to = wide_peer(k)
            pltpu.make_async_remote_copy(
                vel.at[c, to], zin.at[c, z_rows], send_sem.at[0], zin_sem.at[c],
                device_id={"wide": to}, device_id_type=MESH,
            ).start()
            return carry

        lax.fori_loop(0, wide_size - 1, one, 0)

    def send_y(c):
        def one(k, carry):
            to = (narrow + k) % narrow_size
            pltpu.make_async_remote_copy(
                ysrc.at[c, to], yin.at[c, y_rows], send_sem.at[1], yin_sem.at[c],
                device_id={"narrow": to}, device_id_type=MESH,
            ).start()
            return carry

        lax.fori_loop(1, narrow_size, one, 0)

    def return_z(c):
        def one(k, carry):
            to = wide_peer(k)
            pltpu.make_async_remote_copy(
                zres.at[c, pl.ds(pl.multiple_of(to * cols, cols), cols)], zret.at[c, wide], send_sem.at[2], zret_sem.at[c],
                device_id={"wide": to}, device_id_type=MESH,
            ).start()
            return carry

        lax.fori_loop(0, wide_size - 1, one, 0)

    def return_y(c):
        def one(k, carry):
            to = (narrow + k) % narrow_size
            pltpu.make_async_remote_copy(
                yres.at[c, pl.ds(pl.multiple_of(to * rows, rows), rows)], yret.at[c, narrow], send_sem.at[3], yret_sem.at[c],
                device_id={"narrow": to}, device_id_type=MESH,
            ).start()
            return carry

        lax.fori_loop(1, narrow_size, one, 0)

    def lines_up(c):
        for n in range(narrow_size):
            ysrc[c, n] = velv[c, :, n, :]
        yin[c, y_rows] = ysrc[c, narrow]
        zin[c, z_rows] = velv[c, wide]

    send_z(Z_ORDER[0])
    load_vel.wait()
    lines_up(Y_ORDER[0])
    send_y(Y_ORDER[0])
    send_z(Z_ORDER[1])
    lines_up(Y_ORDER[1])
    send_y(Y_ORDER[1])
    send_z(Z_ORDER[2])
    lines_up(Y_ORDER[2])
    send_y(Y_ORDER[2])

    for load in loads:
        load.wait()
    for k in range(2):
        hx[k], lx[k] = split((-0.5, 0.5)[k] * opx[k])
    for k in range(4):
        hyz[k], lyz[k] = split((-0.5, 0.5)[k % 2] * opyz[k])

    def x_part(c, carry):
        along = velv[0].reshape(rows * cols, width)
        field = velv[c].reshape(rows * cols, width)
        pair = split(field)
        total = product_t(split(field * along), (hx[0], lx[0])) + product_t(pair, (hx[1], lx[1]))
        total = total + along * product_t(pair, (hx[0], lx[0]))
        acc[c] = total.reshape(rows, cols, width)
        return carry

    lax.fori_loop(0, 3, x_part, 0)

    def line_part(source, result, operators, direction, c):
        slope, curve = (hyz[operators], lyz[operators]), (hyz[operators + 1], lyz[operators + 1])
        along, field = source[direction], source[c]
        pair = split(field)
        total = product(slope, split(field * along)) + product(curve, pair)
        result[c] = total + along * product(slope, pair)

    def arrived(sem, buffer, blocks, size):
        part = buffer.at[pl.ds(0, (blocks - 1) * size)]
        pltpu.make_async_copy(part, part, sem).wait()

    for step in range(3):
        c = Z_ORDER[step]
        arrived(zin_sem.at[c], zin.at[c], wide_size, cols)
        line_part(zin, zres, 2, 2, c)
        return_z(c)
        zret[c, wide] = zres[c, z_rows]
        c = Y_ORDER[step]
        arrived(yin_sem.at[c], yin.at[c], narrow_size, rows)
        line_part(yin, yres, 0, 1, c)
        return_y(c)
        yret[c, narrow] = yres[c, y_rows]

    for c in Y_ORDER:
        arrived(yret_sem.at[c], yret.at[c], narrow_size, 1)
        for n in range(narrow_size):
            acc[c, :, n, :] = acc[c, :, n, :] + yret[c, n]
    for c in Z_ORDER:
        arrived(zret_sem.at[c], zret.at[c], wide_size, 1)
        acc[c] = acc[c] + zret[c]

    for sem, buffer, blocks, size in (
        (send_sem.at[0], zin, wide_size, cols),
        (send_sem.at[1], yin, narrow_size, rows),
        (send_sem.at[2], zin, wide_size, cols),
        (send_sem.at[3], yin, narrow_size, rows),
    ):
        part = buffer.at[:, pl.ds(0, (blocks - 1) * size)]
        pltpu.make_async_copy(part, part, sem).wait()


def on_device(wide_size, narrow_size, velocity, slope_x, curve_x, slope_y, curve_y, slope_z, curve_z):
    _, rows, cols, width = velocity.shape
    z_lines, y_lines = wide_size * cols, narrow_size * rows
    dma = pltpu.SemaphoreType.DMA
    return pl.pallas_call(
        functools.partial(kernel, wide_size, narrow_size),
        out_shape=jax.ShapeDtypeStruct(velocity.shape, F32),
        in_specs=[pl.BlockSpec(memory_space=pltpu.HBM)] * 7,
        out_specs=pl.BlockSpec(memory_space=pltpu.VMEM),
        scratch_shapes=[
            pltpu.VMEM(velocity.shape, F32),
            pltpu.VMEM((2, width, width), F32),
            pltpu.VMEM((4, z_lines, z_lines), F32),
            pltpu.VMEM((2, width, width), BF16),
            pltpu.VMEM((2, width, width), BF16),
            pltpu.VMEM((4, z_lines, z_lines), BF16),
            pltpu.VMEM((4, z_lines, z_lines), BF16),
            pltpu.VMEM((3, cols, rows, width), F32),
            pltpu.VMEM((3, z_lines, width), F32),
            pltpu.VMEM((3, y_lines, width), F32),
            pltpu.VMEM((3, z_lines, width), F32),
            pltpu.VMEM((3, y_lines, width), F32),
            pltpu.VMEM((3, cols, rows, width), F32),
            pltpu.VMEM(velocity.shape, F32),
            dma((7,)),
            dma((4,)),
            dma((3,)),
            dma((3,)),
            dma((3,)),
            dma((3,)),
        ],
        compiler_params=pltpu.CompilerParams(
            collective_id=0, has_side_effects=True, vmem_limit_bytes=40 * 1024 * 1024
        ),
    )(*[pltpu.with_memory_space_constraint(a, pltpu.HBM) for a in (velocity, slope_x, curve_x, slope_y, curve_y, slope_z, curve_z)])


def solution(mesh):
    return jax.shard_map(
        functools.partial(on_device, mesh.shape["wide"], mesh.shape["narrow"]),
        mesh=mesh,
        in_specs=(P(None, "narrow", "wide", None), P(), P(), P(), P(), P(), P()),
        out_specs=P(None, "narrow", "wide", None),
        check_vma=False,
    )
```

```python
import functools

import jax
import jax.numpy as jnp
from jax import lax
from jax.experimental import pallas as pl
from jax.experimental.pallas import tpu as pltpu
from jax.sharding import PartitionSpec as P

MESH = pl.DeviceIdType.MESH
F32 = jnp.float32
BF16 = jnp.bfloat16


def split(value):
    high = value.astype(BF16)
    return high, (value - high.astype(F32)).astype(BF16)


def product(left, right):
    dot = functools.partial(jnp.dot, preferred_element_type=F32)
    return dot(left[0], right[0]) + (dot(left[0], right[1]) + dot(left[1], right[0]))


def product_t(left, right):
    dot = functools.partial(lax.dot_general, dimension_numbers=(((1,), (1,)), ((), ())), preferred_element_type=F32)
    return dot(left[0], right[0]) + (dot(left[0], right[1]) + dot(left[1], right[0]))


def kernel(
    wide_size, narrow_size,
    vel, sx, cx, sy, cy, sz, cz,
    acc,
    velv, opx, opyz, hx, lx, hyz, lyz,
    pin, qin, ysp, ysq, zin, yin, zres, yres,
    zret_p, zret_o, yret_p, yret_q, psum, back_p, back_q,
    load_sem, send_sem, pin_sem, qin_sem, zin_sem, yin_sem,
    zret_p_sem, zret_o_sem, yret_p_sem, yret_q_sem, back_p_sem, back_q_sem,
):
    wide = lax.axis_index("wide")
    narrow = lax.axis_index("narrow")
    rows, cols, width = velv.shape[1], velv.shape[2], velv.shape[3]
    half = width // 2
    deep, across = wide_size // 4, narrow_size // 2
    group = 2 * deep
    y_lo, place, core = wide // group, wide % group, wide % 2
    z = place // 2
    y_hi, x = narrow // across, narrow % across
    p_wide = (1 - y_lo) * group + place
    q_narrow = (1 - y_hi) * across + x
    p_device = {"wide": p_wide}
    q_device = {"wide": p_wide, "narrow": q_narrow}
    kept = (y_hi + y_lo) % 2
    keep = pl.ds(pl.multiple_of(kept * half, 128), half)
    give = pl.ds(pl.multiple_of((1 - kept) * half, 128), half)
    line_rows, planes = rows // group, cols // across

    def z_peer(k):
        turn = k // 2
        far = (deep // 2 - (turn + 1) // 2) * (1 - 2 * ((turn + 1 + core) % 2))
        return (z + far + deep) % deep * 2 + (core + 1 - k % 2) % 2

    def to_place(place_to):
        return {"wide": y_lo * group + place_to}

    def to_x(x_to):
        return {"narrow": y_hi * across + x_to}

    barrier = pltpu.get_barrier_semaphore()

    def greet(k, carry):
        pl.semaphore_signal(barrier, inc=1, device_id=to_place(z_peer(k)), device_id_type=MESH)
        return carry

    lax.fori_loop(0, group - 1, greet, 0)
    for k in range(1, across):
        pl.semaphore_signal(barrier, inc=1, device_id=to_x((x + k) % across), device_id_type=MESH)
    pl.semaphore_signal(barrier, inc=1, device_id=p_device, device_id_type=MESH)
    pl.semaphore_signal(barrier, inc=1, device_id=q_device, device_id_type=MESH)

    load_vel = pltpu.make_async_copy(vel, velv, load_sem.at[0])
    load_vel.start()
    loads = [
        pltpu.make_async_copy(source, target, load_sem.at[1 + k])
        for k, (source, target) in enumerate(
            [(sx, opx.at[0]), (cx, opx.at[1]), (sy, opyz.at[0]), (cy, opyz.at[1]), (sz, opyz.at[2]), (cz, opyz.at[3])]
        )
    ]
    for load in loads:
        load.start()
    pl.semaphore_wait(barrier, group + across)

    def block(index, size):
        return pl.ds(pl.multiple_of(index * size, size), size)

    def send(source, target, sent, landed, device):
        pltpu.make_async_remote_copy(
            source, target, send_sem.at[sent], landed, device_id=device, device_id_type=MESH
        ).start()

    def each_place(one):
        def step(k, carry):
            one(z_peer(k))
            return carry

        lax.fori_loop(0, group - 1, step, 0)

    def send_p(c):
        send(vel.at[c, :, :, give], pin.at[c], 0, pin_sem.at[c], p_device)

    def send_q(c):
        send(vel.at[c, :, :, keep], qin.at[c], 1, qin_sem.at[c], q_device)

    def send_z_own(c):
        def one(to):
            send(vel.at[c, block(to, line_rows), :, keep], zin.at[c, :, block(wide, cols)], 2, zin_sem.at[c], to_place(to))

        each_place(one)

    def send_z_p(c):
        def one(to):
            send(pin.at[c, block(to, line_rows)], zin.at[c, :, block(p_wide, cols)], 2, zin_sem.at[c], to_place(to))

        each_place(one)
        zin[c, :, block(p_wide, cols)] = pin[c, block(place, line_rows)]

    def send_y(c, source, turned, from_narrow):
        for plane in range(cols):
            turned[c, plane] = source[c, :, plane, :]
        for k in range(1, across):
            to = (x + k) % across
            send(turned.at[c, block(to, planes)], yin.at[c, :, block(from_narrow, rows)], 3, yin_sem.at[c], to_x(to))
        yin[c, :, block(from_narrow, rows)] = turned[c, block(x, planes)]

    def arrived(part, sem):
        pltpu.make_async_copy(part, part, sem).wait()

    def line_part(source, result, operators, direction, c, count):
        slope, curve = (hyz[operators], lyz[operators]), (hyz[operators + 1], lyz[operators + 1])

        def one(k, carry):
            along, field = source[direction, k], source[c, k]
            pair = split(field)
            total = product(slope, split(field * along)) + product(curve, pair)
            result[c, k] = total + along * product(slope, pair)
            return carry

        lax.fori_loop(0, count, one, 0)

    def x_part(c):
        along = velv[0].reshape(rows * cols, width)
        field = velv[c].reshape(rows * cols, width)
        pair = split(field)
        total = product_t(split(field * along), (hx[0], lx[0])) + product_t(pair, (hx[1], lx[1]))
        total = total + along * product_t(pair, (hx[0], lx[0]))
        acc[c] = total.reshape(rows, cols, width)

    def z_part(c):
        arrived(zin.at[c, :, pl.ds(0, 2 * (group - 1) * cols)], zin_sem.at[c])
        line_part(zin, zres, 2, 2, c, line_rows)

        def one_p(to):
            send(zres.at[c, :, block((1 - y_lo) * group + to, cols)], zret_p.at[c, block(place, line_rows)], 4, zret_p_sem.at[c], to_place(to))

        def one_o(to):
            send(zres.at[c, :, block(y_lo * group + to, cols)], zret_o.at[c, block(place, line_rows)], 4, zret_o_sem.at[c], to_place(to))

        each_place(one_p)
        each_place(one_o)
        zret_p[c, block(place, line_rows)] = zres[c, :, block(p_wide, cols)]
        zret_o[c, block(place, line_rows)] = zres[c, :, block(wide, cols)]

    def y_part(c):
        if across > 1:
            arrived(yin.at[c, :, pl.ds(0, 2 * (across - 1) * rows)], yin_sem.at[c])
        line_part(yin, yres, 0, 1, c, planes)
        for k in range(1, across):
            to = (x + k) % across
            send(yres.at[c, :, block((1 - y_hi) * across + to, rows)], yret_q.at[c, block(x, planes)], 5, yret_q_sem.at[c], to_x(to))
        for k in range(1, across):
            to = (x + k) % across
            send(yres.at[c, :, block(y_hi * across + to, rows)], yret_p.at[c, block(x, planes)], 5, yret_p_sem.at[c], to_x(to))
        yret_q[c, block(x, planes)] = yres[c, :, block(q_narrow, rows)]
        yret_p[c, block(x, planes)] = yres[c, :, block(narrow, rows)]

    def back_to_q(c):
        if across > 1:
            arrived(yret_q.at[c, pl.ds(0, (across - 1) * planes)], yret_q_sem.at[c])
        send(yret_q.at[c], back_q.at[c], 6, back_q_sem.at[c], q_device)

    def back_to_p(c):
        if across > 1:
            arrived(yret_p.at[c, pl.ds(0, (across - 1) * planes)], yret_p_sem.at[c])
        arrived(zret_p.at[c, pl.ds(0, (group - 1) * line_rows)], zret_p_sem.at[c])
        for plane in range(cols):
            psum[c, :, plane, :] = zret_p[c, :, plane, :] + yret_p[c, plane]
        send(psum.at[c], back_p.at[c], 7, back_p_sem.at[c], p_device)

    def add_q(c):
        arrived(back_q.at[c], back_q_sem.at[c])
        for plane in range(cols):
            acc[c, :, plane, keep] = acc[c, :, plane, keep] + back_q[c, plane]

    def add_p(c):
        arrived(back_p.at[c], back_p_sem.at[c])
        acc[c, :, :, give] = acc[c, :, :, give] + back_p[c]

    def add_own(c):
        arrived(zret_o.at[c, pl.ds(0, (group - 1) * line_rows)], zret_o_sem.at[c])
        acc[c, :, :, keep] = acc[c, :, :, keep] + zret_o[c]

    send_p(2)
    send_z_own(2)
    send_q(1)
    send_p(1)
    send_z_own(1)
    send_q(2)
    send_p(0)
    send_z_own(0)
    send_q(0)

    load_vel.wait()
    for c in range(3):
        zin[c, :, block(wide, cols)] = velv[c, block(place, line_rows), :, keep]
    for load in loads:
        load.wait()
    for k in range(2):
        hx[k], lx[k] = split((-0.5, 0.5)[k] * opx[k])
    for k in range(4):
        hyz[k], lyz[k] = split((-0.5, 0.5)[k % 2] * opyz[k])

    arrived(pin.at[2], pin_sem.at[2])
    send_z_p(2)
    x_part(2)
    arrived(pin.at[1], pin_sem.at[1])
    send_y(1, pin, ysp, narrow)
    send_z_p(1)
    arrived(qin.at[1], qin_sem.at[1])
    send_y(1, qin, ysq, q_narrow)
    send_y(2, pin, ysp, narrow)
    x_part(1)
    arrived(pin.at[0], pin_sem.at[0])
    send_z_p(0)
    send_y(0, pin, ysp, narrow)
    arrived(qin.at[2], qin_sem.at[2])
    send_y(2, qin, ysq, q_narrow)
    arrived(qin.at[0], qin_sem.at[0])
    send_y(0, qin, ysq, q_narrow)
    x_part(0)

    z_part(2)
    y_part(1)
    y_part(2)
    back_to_q(1)
    z_part(1)
    y_part(0)
    back_to_q(2)
    z_part(0)
    back_to_q(0)
    back_to_p(2)
    add_q(1)
    add_q(2)
    back_to_p(1)
    add_q(0)
    add_p(2)
    add_own(2)
    back_to_p(0)
    add_p(1)
    add_own(1)
    add_p(0)
    add_own(0)

    parts = [pin, qin, zin.at[:, :, pl.ds(0, 2 * (group - 1) * cols)]] * 2
    for k, part in ((0, pin), (1, qin), (2, parts[2]), (4, parts[2]), (6, back_q), (7, back_p)):
        arrived(part, send_sem.at[k])
    if across > 1:
        for k in (3, 5):
            arrived(yin.at[:, :, pl.ds(0, 2 * (across - 1) * rows)], send_sem.at[k])


def on_device(wide_size, narrow_size, *arrays):
    shape = arrays[0].shape
    _, rows, cols, width = shape
    group, across, half = wide_size // 2, narrow_size // 2, width // 2
    z_lines, y_lines = wide_size * cols, narrow_size * rows
    vmem, dma = pltpu.VMEM, pltpu.SemaphoreType.DMA
    part, turned = vmem((3, rows, cols, half), F32), vmem((3, cols, rows, half), F32)
    z_block, y_block = vmem((3, rows // group, z_lines, half), F32), vmem((3, cols // across, y_lines, half), F32)
    return pl.pallas_call(
        functools.partial(kernel, wide_size, narrow_size),
        out_shape=jax.ShapeDtypeStruct(shape, F32),
        in_specs=[pl.BlockSpec(memory_space=pltpu.HBM)] * 7,
        out_specs=pl.BlockSpec(memory_space=pltpu.VMEM),
        scratch_shapes=[
            vmem(shape, F32),
            vmem((2, width, width), F32),
            vmem((4, z_lines, z_lines), F32),
            vmem((2, width, width), BF16),
            vmem((2, width, width), BF16),
            vmem((4, z_lines, z_lines), BF16),
            vmem((4, z_lines, z_lines), BF16),
            part, part, turned, turned, z_block, y_block, z_block, y_block,
            part, part, turned, turned, part, part, turned,
            dma((7,)),
            dma((8,)),
            *[dma((3,))] * 10,
        ],
        compiler_params=pltpu.CompilerParams(
            collective_id=0, has_side_effects=True, vmem_limit_bytes=40 * 1024 * 1024
        ),
    )(*[pltpu.with_memory_space_constraint(array, pltpu.HBM) for array in arrays])


def solution(mesh):
    return jax.shard_map(
        functools.partial(on_device, mesh.shape["wide"], mesh.shape["narrow"]),
        mesh=mesh,
        in_specs=(P(None, "narrow", "wide", None), P(), P(), P(), P(), P(), P()),
        out_specs=P(None, "narrow", "wide", None),
        check_vma=False,
    )
```

```python
import functools

import jax
import jax.numpy as jnp
from jax import lax
from jax.experimental import pallas as pl
from jax.experimental.pallas import tpu as pltpu
from jax.sharding import PartitionSpec as P

MESH = pl.DeviceIdType.MESH
F32 = jnp.float32
BF16 = jnp.bfloat16


def split(value):
    high = value.astype(BF16)
    return high, (value - high.astype(F32)).astype(BF16)


def product(left, right):
    dot = functools.partial(jnp.dot, preferred_element_type=F32)
    return dot(left[0], right[0]) + (dot(left[0], right[1]) + dot(left[1], right[0]))


def product_t(left, right):
    dot = functools.partial(lax.dot_general, dimension_numbers=(((1,), (1,)), ((), ())), preferred_element_type=F32)
    return dot(left[0], right[0]) + (dot(left[0], right[1]) + dot(left[1], right[0]))


def kernel(
    wide_size, narrow_size,
    vel, sx, cx, sy, cy, sz, cz,
    acc,
    velv, opx, opyz, hx, lx, hyz, lyz,
    pin, qin, ysp, ysq, zin, yin, zres, yres,
    zret_p, zret_o, yret_p, yret_q, psum, back_p, back_q,
    load_sem, send_sem, pin_sem, qin_sem, zin_sem, yin_sem,
    zret_p_sem, zret_o_sem, yret_p_sem, yret_q_sem, back_p_sem, back_q_sem,
):
    wide = lax.axis_index("wide")
    narrow = lax.axis_index("narrow")
    rows, cols, width = velv.shape[1], velv.shape[2], velv.shape[3]
    half = width // 2
    deep, across = wide_size // 4, narrow_size // 2
    group = 2 * deep
    y_lo, place, core = wide // group, wide % group, wide % 2
    z = place // 2
    y_hi, x = narrow // across, narrow % across
    p_wide = (1 - y_lo) * group + place
    q_narrow = (1 - y_hi) * across + x
    p_device = {"wide": p_wide}
    q_device = {"wide": p_wide, "narrow": q_narrow}
    kept = (y_hi + y_lo) % 2
    keep = pl.ds(pl.multiple_of(kept * half, 128), half)
    give = pl.ds(pl.multiple_of((1 - kept) * half, 128), half)
    line_rows, planes = rows // group, cols // across

    def z_peer(k):
        turn = k // 2
        far = (deep // 2 - (turn + 1) // 2) * (1 - 2 * ((turn + 1 + core) % 2))
        return (z + far + deep) % deep * 2 + (core + 1 - k % 2) % 2

    def to_place(place_to):
        return {"wide": y_lo * group + place_to}

    def to_x(x_to):
        return {"narrow": y_hi * across + x_to}

    barrier = pltpu.get_barrier_semaphore()

    for k in range(group - 1):
        pl.semaphore_signal(barrier, inc=1, device_id=to_place(z_peer(k)), device_id_type=MESH)
    for k in range(1, across):
        pl.semaphore_signal(barrier, inc=1, device_id=to_x((x + k) % across), device_id_type=MESH)
    pl.semaphore_signal(barrier, inc=1, device_id=p_device, device_id_type=MESH)
    pl.semaphore_signal(barrier, inc=1, device_id=q_device, device_id_type=MESH)

    load_vel = pltpu.make_async_copy(vel, velv, load_sem.at[0])
    load_vel.start()
    loads = [
        pltpu.make_async_copy(source, target, load_sem.at[1 + k])
        for k, (source, target) in enumerate(
            [(sx, opx.at[0]), (cx, opx.at[1]), (sy, opyz.at[0]), (cy, opyz.at[1]), (sz, opyz.at[2]), (cz, opyz.at[3])]
        )
    ]
    for load in loads:
        load.start()
    pl.semaphore_wait(barrier, group + across)

    def block(index, size):
        return pl.ds(pl.multiple_of(index * size, size), size)

    def send(source, target, sent, landed, device):
        pltpu.make_async_remote_copy(
            source, target, send_sem.at[sent], landed, device_id=device, device_id_type=MESH
        ).start()

    def each_place(one):
        def step(k, carry):
            one(z_peer(k))
            return carry

        lax.fori_loop(0, group - 1, step, 0)

    def send_out(c, q_c):
        def pieces(k):
            part = block(k, line_rows)
            send(vel.at[c, part, :, give], pin.at[c, part], 0, pin_sem.at[c], p_device)
            send(vel.at[q_c, part, :, keep], qin.at[q_c, part], 1, qin_sem.at[q_c], q_device)

        def step(k, carry):
            to = z_peer(k)
            send(vel.at[c, block(to, line_rows), :, keep], zin.at[c, :, block(wide, cols)], 2, zin_sem.at[c], to_place(to))
            pieces(k)
            return carry

        lax.fori_loop(0, group - 1, step, 0)
        pieces(group - 1)

    def send_z_p(c):
        def one(to):
            send(pin.at[c, block(to, line_rows)], zin.at[c, :, block(p_wide, cols)], 2, zin_sem.at[c], to_place(to))

        each_place(one)
        zin[c, :, block(p_wide, cols)] = pin[c, block(place, line_rows)]

    def send_y(c, source, turned, from_narrow):
        for plane in range(cols):
            turned[c, plane] = source[c, :, plane, :]
        for k in range(1, across):
            to = (x + k) % across
            send(turned.at[c, block(to, planes)], yin.at[c, :, block(from_narrow, rows)], 3, yin_sem.at[c], to_x(to))
        yin[c, :, block(from_narrow, rows)] = turned[c, block(x, planes)]

    def arrived(part, sem):
        pltpu.make_async_copy(part, part, sem).wait()

    def line_part(source, result, operators, direction, c, count):
        slope, curve = (hyz[operators], lyz[operators]), (hyz[operators + 1], lyz[operators + 1])

        def one(k, carry):
            along, field = source[direction, k], source[c, k]
            pair = split(field)
            total = product(slope, split(field * along)) + product(curve, pair)
            result[c, k] = total + along * product(slope, pair)
            return carry

        lax.fori_loop(0, count, one, 0)

    def x_part(c):
        along = velv[0].reshape(rows * cols, width)
        field = velv[c].reshape(rows * cols, width)
        pair = split(field)
        total = product_t(split(field * along), (hx[0], lx[0])) + product_t(pair, (hx[1], lx[1]))
        total = total + along * product_t(pair, (hx[0], lx[0]))
        acc[c] = total.reshape(rows, cols, width)

    def z_part(c):
        arrived(zin.at[c, :, pl.ds(0, 2 * (group - 1) * cols)], zin_sem.at[c])
        line_part(zin, zres, 2, 2, c, line_rows)

        def one(to):
            send(zres.at[c, :, block((1 - y_lo) * group + to, cols)], zret_p.at[c, block(place, line_rows)], 4, zret_p_sem.at[c], to_place(to))

        each_place(one)
        zret_p[c, block(place, line_rows)] = zres[c, :, block(p_wide, cols)]

    def return_own(c):
        def one(to):
            send(zres.at[c, :, block(y_lo * group + to, cols)], zret_o.at[c, block(place, line_rows)], 4, zret_o_sem.at[c], to_place(to))

        each_place(one)
        zret_o[c, block(place, line_rows)] = zres[c, :, block(wide, cols)]

    def y_part(c):
        if across > 1:
            arrived(yin.at[c, :, pl.ds(0, 2 * (across - 1) * rows)], yin_sem.at[c])
        line_part(yin, yres, 0, 1, c, planes)
        for k in range(1, across):
            to = (x + k) % across
            send(yres.at[c, :, block((1 - y_hi) * across + to, rows)], yret_q.at[c, block(x, planes)], 5, yret_q_sem.at[c], to_x(to))
        for k in range(1, across):
            to = (x + k) % across
            send(yres.at[c, :, block(y_hi * across + to, rows)], yret_p.at[c, block(x, planes)], 5, yret_p_sem.at[c], to_x(to))
        yret_q[c, block(x, planes)] = yres[c, :, block(q_narrow, rows)]
        yret_p[c, block(x, planes)] = yres[c, :, block(narrow, rows)]

    def back_to_q(c):
        if across > 1:
            arrived(yret_q.at[c, pl.ds(0, (across - 1) * planes)], yret_q_sem.at[c])
        send(yret_q.at[c], back_q.at[c], 6, back_q_sem.at[c], q_device)

    def back_to_p(c):
        if across > 1:
            arrived(yret_p.at[c, pl.ds(0, (across - 1) * planes)], yret_p_sem.at[c])
        arrived(zret_p.at[c, pl.ds(0, (group - 1) * line_rows)], zret_p_sem.at[c])
        for plane in range(cols):
            psum[c, :, plane, :] = zret_p[c, :, plane, :] + yret_p[c, plane]
        send(psum.at[c], back_p.at[c], 7, back_p_sem.at[c], p_device)

    def add_q(c):
        arrived(back_q.at[c], back_q_sem.at[c])
        for plane in range(cols):
            acc[c, :, plane, keep] = acc[c, :, plane, keep] + back_q[c, plane]

    def add_p(c):
        arrived(back_p.at[c], back_p_sem.at[c])
        acc[c, :, :, give] = acc[c, :, :, give] + back_p[c]

    def add_own(c):
        arrived(zret_o.at[c, pl.ds(0, (group - 1) * line_rows)], zret_o_sem.at[c])
        acc[c, :, :, keep] = acc[c, :, :, keep] + zret_o[c]

    send_out(2, 1)
    send_out(1, 2)
    send_out(0, 0)

    load_vel.wait()
    for c in range(3):
        zin[c, :, block(wide, cols)] = velv[c, block(place, line_rows), :, keep]
    for load in loads:
        load.wait()
    for k in range(2):
        hx[k], lx[k] = split((-0.5, 0.5)[k] * opx[k])
    for k in range(4):
        hyz[k], lyz[k] = split((-0.5, 0.5)[k % 2] * opyz[k])

    arrived(pin.at[2], pin_sem.at[2])
    send_z_p(2)
    x_part(2)
    arrived(pin.at[1], pin_sem.at[1])
    send_y(1, pin, ysp, narrow)
    send_z_p(1)
    arrived(qin.at[1], qin_sem.at[1])
    send_y(1, qin, ysq, q_narrow)
    send_y(2, pin, ysp, narrow)
    x_part(1)
    arrived(pin.at[0], pin_sem.at[0])
    send_z_p(0)
    send_y(0, pin, ysp, narrow)
    arrived(qin.at[2], qin_sem.at[2])
    send_y(2, qin, ysq, q_narrow)
    arrived(qin.at[0], qin_sem.at[0])
    send_y(0, qin, ysq, q_narrow)
    x_part(0)

    z_part(2)
    return_own(2)
    y_part(1)
    y_part(2)
    back_to_q(1)
    z_part(1)
    y_part(0)
    back_to_q(2)
    z_part(0)
    return_own(1)
    back_to_q(0)
    back_to_p(2)
    add_q(1)
    add_q(2)
    back_to_p(1)
    add_q(0)
    back_to_p(0)
    return_own(0)
    add_p(2)
    add_own(2)
    add_p(1)
    add_own(1)
    add_p(0)
    add_own(0)

    z_blocks = zin.at[:, :, pl.ds(0, 2 * (group - 1) * cols)]
    for k, part in ((0, pin), (1, qin), (2, z_blocks), (4, z_blocks), (6, back_q), (7, back_p)):
        arrived(part, send_sem.at[k])
    if across > 1:
        for k in (3, 5):
            arrived(yin.at[:, :, pl.ds(0, 2 * (across - 1) * rows)], send_sem.at[k])


def on_device(wide_size, narrow_size, *arrays):
    shape = arrays[0].shape
    _, rows, cols, width = shape
    group, across, half = wide_size // 2, narrow_size // 2, width // 2
    z_lines, y_lines = wide_size * cols, narrow_size * rows
    vmem, dma = pltpu.VMEM, pltpu.SemaphoreType.DMA
    part, turned = vmem((3, rows, cols, half), F32), vmem((3, cols, rows, half), F32)
    z_block, y_block = vmem((3, rows // group, z_lines, half), F32), vmem((3, cols // across, y_lines, half), F32)
    return pl.pallas_call(
        functools.partial(kernel, wide_size, narrow_size),
        out_shape=jax.ShapeDtypeStruct(shape, F32),
        in_specs=[pl.BlockSpec(memory_space=pltpu.HBM)] * 7,
        out_specs=pl.BlockSpec(memory_space=pltpu.VMEM),
        scratch_shapes=[
            vmem(shape, F32),
            vmem((2, width, width), F32),
            vmem((4, z_lines, z_lines), F32),
            vmem((2, width, width), BF16),
            vmem((2, width, width), BF16),
            vmem((4, z_lines, z_lines), BF16),
            vmem((4, z_lines, z_lines), BF16),
            part, part, turned, turned, z_block, y_block, z_block, y_block,
            part, part, turned, turned, part, part, turned,
            dma((7,)),
            dma((8,)),
            *[dma((3,))] * 10,
        ],
        compiler_params=pltpu.CompilerParams(
            collective_id=0, has_side_effects=True, vmem_limit_bytes=40 * 1024 * 1024
        ),
    )(*[pltpu.with_memory_space_constraint(array, pltpu.HBM) for array in arrays])


def solution(mesh):
    return jax.shard_map(
        functools.partial(on_device, mesh.shape["wide"], mesh.shape["narrow"]),
        mesh=mesh,
        in_specs=(P(None, "narrow", "wide", None), P(), P(), P(), P(), P(), P()),
        out_specs=P(None, "narrow", "wide", None),
        check_vma=False,
    )
```

```python
import functools

import jax
import jax.numpy as jnp
from jax import lax
from jax.experimental import pallas as pl
from jax.experimental.pallas import tpu as pltpu
from jax.sharding import PartitionSpec as P

MESH = pl.DeviceIdType.MESH
F32 = jnp.float32
BF16 = jnp.bfloat16


def split(value):
    high = value.astype(BF16)
    return high, (value - high.astype(F32)).astype(BF16)


def product(left, right):
    dot = functools.partial(jnp.dot, preferred_element_type=F32)
    return dot(left[0], right[0]) + (dot(left[0], right[1]) + dot(left[1], right[0]))


def product_t(left, right):
    dot = functools.partial(lax.dot_general, dimension_numbers=(((1,), (1,)), ((), ())), preferred_element_type=F32)
    return dot(left[0], right[0]) + (dot(left[0], right[1]) + dot(left[1], right[0]))


def kernel(
    wide_size, narrow_size,
    vel, sx, cx, sy, cy, sz, cz,
    acc,
    velv, opx, opyz, hx, lx, hyz, lyz,
    pin, qin, ysp, ysq, zin, yin, zres, yres,
    zret_p, zret_o, yret_p, yret_q, psum, back_p, back_q,
    load_sem, send_sem, pin_sem, qin_sem, zin_sem, yin_sem,
    zret_p_sem, zret_o_sem, yret_p_sem, yret_q_sem, back_p_sem, back_q_sem,
):
    wide = lax.axis_index("wide")
    narrow = lax.axis_index("narrow")
    rows, cols, width = velv.shape[1], velv.shape[2], velv.shape[3]
    half = width // 2
    deep, across = wide_size // 4, narrow_size // 2
    group = 2 * deep
    y_lo, place, core = wide // group, wide % group, wide % 2
    z = place // 2
    y_hi, x = narrow // across, narrow % across
    p_wide = (1 - y_lo) * group + place
    q_narrow = (1 - y_hi) * across + x
    p_device = {"wide": p_wide}
    q_device = {"wide": p_wide, "narrow": q_narrow}
    kept = (y_hi + y_lo) % 2
    keep = pl.ds(pl.multiple_of(kept * half, 128), half)
    give = pl.ds(pl.multiple_of((1 - kept) * half, 128), half)
    line_rows, planes = rows // group, cols // across

    def z_peer(k):
        turn = k // 2
        far = (deep // 2 - (turn + 1) // 2) * (1 - 2 * ((turn + 1 + core) % 2))
        return (z + far + deep) % deep * 2 + (core + 1 - k % 2) % 2

    def to_place(place_to):
        return {"wide": y_lo * group + place_to}

    def to_x(x_to):
        return {"narrow": y_hi * across + x_to}

    barrier = pltpu.get_barrier_semaphore()

    for k in range(group - 1):
        pl.semaphore_signal(barrier, inc=1, device_id=to_place(z_peer(k)), device_id_type=MESH)
    for k in range(1, across):
        pl.semaphore_signal(barrier, inc=1, device_id=to_x((x + k) % across), device_id_type=MESH)
    pl.semaphore_signal(barrier, inc=1, device_id=p_device, device_id_type=MESH)
    pl.semaphore_signal(barrier, inc=1, device_id=q_device, device_id_type=MESH)

    load_vel = pltpu.make_async_copy(vel, velv, load_sem.at[0])
    load_vel.start()
    loads = [
        pltpu.make_async_copy(source, target, load_sem.at[1 + k])
        for k, (source, target) in enumerate(
            [(sx, opx.at[0]), (cx, opx.at[1]), (sy, opyz.at[0]), (cy, opyz.at[1]), (sz, opyz.at[2]), (cz, opyz.at[3])]
        )
    ]
    for load in loads:
        load.start()
    pl.semaphore_wait(barrier, group + across)

    def block(index, size):
        return pl.ds(pl.multiple_of(index * size, size), size)

    def send(source, target, sent, landed, device):
        pltpu.make_async_remote_copy(
            source, target, send_sem.at[sent], landed, device_id=device, device_id_type=MESH
        ).start()

    def each_place(one):
        def step(k, carry):
            one(z_peer(k))
            return carry

        lax.fori_loop(0, group - 1, step, 0)

    def send_out(c, q_c):
        def pieces(k):
            part = block(k, line_rows)
            send(vel.at[c, part, :, give], pin.at[c, part], 0, pin_sem.at[c], p_device)
            send(vel.at[q_c, part, :, keep], qin.at[q_c, part], 1, qin_sem.at[q_c], q_device)

        def step(k, carry):
            to = z_peer(k)
            send(vel.at[c, block(to, line_rows), :, keep], zin.at[c, :, block(wide, cols)], 2, zin_sem.at[c], to_place(to))
            pieces(k)
            return carry

        lax.fori_loop(0, group - 1, step, 0)
        pieces(group - 1)

    def send_z_p(c):
        def one(to):
            send(pin.at[c, block(to, line_rows)], zin.at[c, :, block(p_wide, cols)], 2, zin_sem.at[c], to_place(to))

        each_place(one)
        zin[c, :, block(p_wide, cols)] = pin[c, block(place, line_rows)]

    def send_y(c, source, turned, from_narrow):
        for plane in range(cols):
            turned[c, plane] = source[c, :, plane, :]
        for k in range(1, across):
            to = (x + k) % across
            send(turned.at[c, block(to, planes)], yin.at[c, :, block(from_narrow, rows)], 3, yin_sem.at[c], to_x(to))
        yin[c, :, block(from_narrow, rows)] = turned[c, block(x, planes)]

    def arrived(part, sem):
        pltpu.make_async_copy(part, part, sem).wait()

    def line_part(source, result, operators, direction, c, count):
        slope, curve = (hyz[operators], lyz[operators]), (hyz[operators + 1], lyz[operators + 1])

        def one(k, carry):
            along, field = source[direction, k], source[c, k]
            pair = split(field)
            total = product(slope, split(field * along)) + product(curve, pair)
            result[c, k] = total + along * product(slope, pair)
            return carry

        lax.fori_loop(0, count, one, 0)

    def x_part(c):
        along = velv[0].reshape(rows * cols, width)
        field = velv[c].reshape(rows * cols, width)
        pair = split(field)
        total = product_t(split(field * along), (hx[0], lx[0])) + product_t(pair, (hx[1], lx[1]))
        total = total + along * product_t(pair, (hx[0], lx[0]))
        acc[c] = total.reshape(rows, cols, width)

    def z_part(c):
        arrived(zin.at[c, :, pl.ds(0, 2 * (group - 1) * cols)], zin_sem.at[c])
        line_part(zin, zres, 2, 2, c, line_rows)

        def one(to):
            send(zres.at[c, :, block((1 - y_lo) * group + to, cols)], zret_p.at[c, block(place, line_rows)], 4, zret_p_sem.at[c], to_place(to))

        each_place(one)
        zret_p[c, block(place, line_rows)] = zres[c, :, block(p_wide, cols)]

    def return_own_low_first(c, first, count):
        def step(j, carry):
            to = (j // deep * (deep // 2) + (z + j % deep // 2) % (deep // 2)) * 2 + (core + 1 - j % 2) % 2

            @pl.when(to != place)
            def _():
                send(zres.at[c, :, block(y_lo * group + to, cols)], zret_o.at[c, block(place, line_rows)], 4, zret_o_sem.at[c], to_place(to))

            return carry

        lax.fori_loop(first, first + count, step, 0)

    def return_own(c):
        def one(to):
            send(zres.at[c, :, block(y_lo * group + to, cols)], zret_o.at[c, block(place, line_rows)], 4, zret_o_sem.at[c], to_place(to))

        each_place(one)
        zret_o[c, block(place, line_rows)] = zres[c, :, block(wide, cols)]

    def y_part(c):
        if across > 1:
            arrived(yin.at[c, :, pl.ds(0, 2 * (across - 1) * rows)], yin_sem.at[c])
        line_part(yin, yres, 0, 1, c, planes)
        for k in range(1, across):
            to = (x + k) % across
            send(yres.at[c, :, block((1 - y_hi) * across + to, rows)], yret_q.at[c, block(x, planes)], 5, yret_q_sem.at[c], to_x(to))
        for k in range(1, across):
            to = (x + k) % across
            send(yres.at[c, :, block(y_hi * across + to, rows)], yret_p.at[c, block(x, planes)], 5, yret_p_sem.at[c], to_x(to))
        yret_q[c, block(x, planes)] = yres[c, :, block(q_narrow, rows)]
        yret_p[c, block(x, planes)] = yres[c, :, block(narrow, rows)]

    def back_to_q(c):
        if across > 1:
            arrived(yret_q.at[c, pl.ds(0, (across - 1) * planes)], yret_q_sem.at[c])
        send(yret_q.at[c], back_q.at[c], 6, back_q_sem.at[c], q_device)

    def back_to_p(c):
        if across > 1:
            arrived(yret_p.at[c, pl.ds(0, (across - 1) * planes)], yret_p_sem.at[c])
        arrived(zret_p.at[c, pl.ds(0, (group - 1) * line_rows)], zret_p_sem.at[c])
        for plane in range(cols):
            psum[c, :, plane, :] = zret_p[c, :, plane, :] + yret_p[c, plane]
        send(psum.at[c], back_p.at[c], 7, back_p_sem.at[c], p_device)

    def add_q(c):
        arrived(back_q.at[c], back_q_sem.at[c])
        for plane in range(cols):
            acc[c, :, plane, keep] = acc[c, :, plane, keep] + back_q[c, plane]

    def add_p(c):
        arrived(back_p.at[c], back_p_sem.at[c])
        acc[c, :, :, give] = acc[c, :, :, give] + back_p[c]

    def add_own(c):
        arrived(zret_o.at[c, pl.ds(0, (group - 1) * line_rows)], zret_o_sem.at[c])
        acc[c, :, :, keep] = acc[c, :, :, keep] + zret_o[c]

    send_out(2, 1)
    send_out(1, 2)
    send_out(0, 0)

    load_vel.wait()
    for c in range(3):
        zin[c, :, block(wide, cols)] = velv[c, block(place, line_rows), :, keep]
    for load in loads:
        load.wait()
    for k in range(2):
        hx[k], lx[k] = split((-0.5, 0.5)[k] * opx[k])
    for k in range(4):
        hyz[k], lyz[k] = split((-0.5, 0.5)[k % 2] * opyz[k])

    arrived(pin.at[2], pin_sem.at[2])
    send_z_p(2)
    x_part(2)
    arrived(pin.at[1], pin_sem.at[1])
    send_y(1, pin, ysp, narrow)
    send_z_p(1)
    arrived(qin.at[1], qin_sem.at[1])
    send_y(1, qin, ysq, q_narrow)
    send_y(2, pin, ysp, narrow)
    x_part(1)
    arrived(pin.at[0], pin_sem.at[0])
    send_z_p(0)
    send_y(0, pin, ysp, narrow)
    arrived(qin.at[2], qin_sem.at[2])
    send_y(2, qin, ysq, q_narrow)
    arrived(qin.at[0], qin_sem.at[0])
    send_y(0, qin, ysq, q_narrow)
    x_part(0)

    z_part(2)
    return_own(2)
    y_part(1)
    y_part(2)
    back_to_q(1)
    z_part(1)
    y_part(0)
    back_to_q(2)
    z_part(0)
    return_own(1)
    back_to_q(0)
    back_to_p(2)
    add_q(1)
    add_q(2)
    back_to_p(1)
    add_q(0)
    back_to_p(0)
    return_own_low_first(0, 0, group)
    zret_o[0, block(place, line_rows)] = zres[0, :, block(wide, cols)]
    add_p(2)
    add_own(2)
    add_p(1)
    add_own(1)
    add_p(0)
    add_own(0)

    z_blocks = zin.at[:, :, pl.ds(0, 2 * (group - 1) * cols)]
    for k, part in ((0, pin), (1, qin), (2, z_blocks), (4, z_blocks), (6, back_q), (7, back_p)):
        arrived(part, send_sem.at[k])
    if across > 1:
        for k in (3, 5):
            arrived(yin.at[:, :, pl.ds(0, 2 * (across - 1) * rows)], send_sem.at[k])


def on_device(wide_size, narrow_size, *arrays):
    shape = arrays[0].shape
    _, rows, cols, width = shape
    group, across, half = wide_size // 2, narrow_size // 2, width // 2
    z_lines, y_lines = wide_size * cols, narrow_size * rows
    vmem, dma = pltpu.VMEM, pltpu.SemaphoreType.DMA
    part, turned = vmem((3, rows, cols, half), F32), vmem((3, cols, rows, half), F32)
    z_block, y_block = vmem((3, rows // group, z_lines, half), F32), vmem((3, cols // across, y_lines, half), F32)
    return pl.pallas_call(
        functools.partial(kernel, wide_size, narrow_size),
        out_shape=jax.ShapeDtypeStruct(shape, F32),
        in_specs=[pl.BlockSpec(memory_space=pltpu.HBM)] * 7,
        out_specs=pl.BlockSpec(memory_space=pltpu.VMEM),
        scratch_shapes=[
            vmem(shape, F32),
            vmem((2, width, width), F32),
            vmem((4, z_lines, z_lines), F32),
            vmem((2, width, width), BF16),
            vmem((2, width, width), BF16),
            vmem((4, z_lines, z_lines), BF16),
            vmem((4, z_lines, z_lines), BF16),
            part, part, turned, turned, z_block, y_block, z_block, y_block,
            part, part, turned, turned, part, part, turned,
            dma((7,)),
            dma((8,)),
            *[dma((3,))] * 10,
        ],
        compiler_params=pltpu.CompilerParams(
            collective_id=0, has_side_effects=True, vmem_limit_bytes=40 * 1024 * 1024
        ),
    )(*[pltpu.with_memory_space_constraint(array, pltpu.HBM) for array in arrays])


def solution(mesh):
    return jax.shard_map(
        functools.partial(on_device, mesh.shape["wide"], mesh.shape["narrow"]),
        mesh=mesh,
        in_specs=(P(None, "narrow", "wide", None), P(), P(), P(), P(), P(), P()),
        out_specs=P(None, "narrow", "wide", None),
        check_vma=False,
    )
```

```python
import functools

import jax
import jax.numpy as jnp
from jax import lax
from jax.experimental import pallas as pl
from jax.experimental.pallas import tpu as pltpu
from jax.sharding import PartitionSpec as P

MESH = pl.DeviceIdType.MESH
F32 = jnp.float32
BF16 = jnp.bfloat16


def split(value):
    high = value.astype(BF16)
    return high, (value - high.astype(F32)).astype(BF16)


def product(left, right):
    dot = functools.partial(jnp.dot, preferred_element_type=F32)
    return dot(left[0], right[0]) + (dot(left[0], right[1]) + dot(left[1], right[0]))


def product_t(left, right):
    dot = functools.partial(lax.dot_general, dimension_numbers=(((1,), (1,)), ((), ())), preferred_element_type=F32)
    return dot(left[0], right[0]) + (dot(left[0], right[1]) + dot(left[1], right[0]))


def kernel(
    wide_size, narrow_size,
    vel, sx, cx, sy, cy, sz, cz,
    acc,
    velv, opx, opyz, hx, lx, hyz, lyz,
    pin, qin, ysp, ysq, zin, yin, zres, yres,
    zret_p, zret_o, yret_p, yret_q, psum, back_p, back_q,
    load_sem, send_sem, pin_sem, qin_sem, zin_sem, yin_sem,
    zret_p_sem, zret_o_sem, yret_p_sem, yret_q_sem, back_p_sem, back_q_sem, half_sem,
):
    wide = lax.axis_index("wide")
    narrow = lax.axis_index("narrow")
    rows, cols, width = velv.shape[1], velv.shape[2], velv.shape[3]
    half = width // 2
    deep, across = wide_size // 4, narrow_size // 2
    group = 2 * deep
    y_lo, place, core = wide // group, wide % group, wide % 2
    z = place // 2
    y_hi, x = narrow // across, narrow % across
    p_wide = (1 - y_lo) * group + place
    q_narrow = (1 - y_hi) * across + x
    p_device = {"wide": p_wide}
    q_device = {"wide": p_wide, "narrow": q_narrow}
    kept = (y_hi + y_lo) % 2
    keep = pl.ds(pl.multiple_of(kept * half, 128), half)
    give = pl.ds(pl.multiple_of((1 - kept) * half, 128), half)
    line_rows, planes = rows // group, cols // across

    def z_peer(k):
        turn = k // 2
        far = (deep // 2 - (turn + 1) // 2) * (1 - 2 * ((turn + 1 + core) % 2))
        return (z + far + deep) % deep * 2 + (core + 1 - k % 2) % 2

    def to_place(place_to):
        return {"wide": y_lo * group + place_to}

    def to_x(x_to):
        return {"narrow": y_hi * across + x_to}

    barrier = pltpu.get_barrier_semaphore()

    for k in range(group - 1):
        pl.semaphore_signal(barrier, inc=1, device_id=to_place(z_peer(k)), device_id_type=MESH)
    for k in range(1, across):
        pl.semaphore_signal(barrier, inc=1, device_id=to_x((x + k) % across), device_id_type=MESH)
    pl.semaphore_signal(barrier, inc=1, device_id=p_device, device_id_type=MESH)
    pl.semaphore_signal(barrier, inc=1, device_id=q_device, device_id_type=MESH)

    load_vel = pltpu.make_async_copy(vel, velv, load_sem.at[0])
    load_vel.start()
    loads = [
        pltpu.make_async_copy(source, target, load_sem.at[1 + k])
        for k, (source, target) in enumerate(
            [(sx, opx.at[0]), (cx, opx.at[1]), (sy, opyz.at[0]), (cy, opyz.at[1]), (sz, opyz.at[2]), (cz, opyz.at[3])]
        )
    ]
    for load in loads:
        load.start()
    pl.semaphore_wait(barrier, group + across)

    def block(index, size):
        return pl.ds(pl.multiple_of(index * size, size), size)

    def send(source, target, sent, landed, device):
        pltpu.make_async_remote_copy(
            source, target, send_sem.at[sent], landed, device_id=device, device_id_type=MESH
        ).start()

    def each_place(one):
        def step(k, carry):
            one(z_peer(k))
            return carry

        lax.fori_loop(0, group - 1, step, 0)

    def send_out(c, q_c):
        def pieces(k):
            part = block(k, line_rows)
            send(vel.at[c, part, :, give], pin.at[c, part], 0, pin_sem.at[c], p_device)
            send(vel.at[q_c, part, :, keep], qin.at[q_c, part], 1, qin_sem.at[q_c], q_device)

        def step(k, carry):
            to = z_peer(k)
            send(vel.at[c, block(to, line_rows), :, keep], zin.at[c, :, block(wide, cols)], 2, zin_sem.at[c], to_place(to))
            pieces(k)
            return carry

        lax.fori_loop(0, group - 1, step, 0)
        pieces(group - 1)

    def send_z_p(c):
        def one(to):
            send(pin.at[c, block(to, line_rows)], zin.at[c, :, block(p_wide, cols)], 2, zin_sem.at[c], to_place(to))

        each_place(one)
        zin[c, :, block(p_wide, cols)] = pin[c, block(place, line_rows)]

    def send_y(c, source, turned, from_narrow):
        for plane in range(cols):
            turned[c, plane] = source[c, :, plane, :]
        for k in range(1, across):
            to = (x + k) % across
            send(turned.at[c, block(to, planes)], yin.at[c, :, block(from_narrow, rows)], 3, yin_sem.at[c], to_x(to))
        yin[c, :, block(from_narrow, rows)] = turned[c, block(x, planes)]

    def arrived(part, sem):
        pltpu.make_async_copy(part, part, sem).wait()

    def line_part(source, result, operators, direction, c, count):
        slope, curve = (hyz[operators], lyz[operators]), (hyz[operators + 1], lyz[operators + 1])

        def one(k, carry):
            along, field = source[direction, k], source[c, k]
            pair = split(field)
            total = product(slope, split(field * along)) + product(curve, pair)
            result[c, k] = total + along * product(slope, pair)
            return carry

        lax.fori_loop(0, count, one, 0)

    def x_part(c):
        along = velv[0].reshape(rows * cols, width)
        field = velv[c].reshape(rows * cols, width)
        pair = split(field)
        total = product_t(split(field * along), (hx[0], lx[0])) + product_t(pair, (hx[1], lx[1]))
        total = total + along * product_t(pair, (hx[0], lx[0]))
        acc[c] = total.reshape(rows, cols, width)

    def z_part(c):
        arrived(zin.at[c, :, pl.ds(0, 2 * (group - 1) * cols)], zin_sem.at[c])
        line_part(zin, zres, 2, 2, c, line_rows)

        def one(to):
            apart = to // deep - place // deep
            landed = half_sem.at[apart * apart] if c == 0 else zret_p_sem.at[c]
            send(zres.at[c, :, block((1 - y_lo) * group + to, cols)], zret_p.at[c, block(place, line_rows)], 4, landed, to_place(to))

        each_place(one)
        zret_p[c, block(place, line_rows)] = zres[c, :, block(p_wide, cols)]

    def return_own_low_first(c, first, count):
        def step(j, carry):
            to = (j // deep * (deep // 2) + (z + j % deep // 2) % (deep // 2)) * 2 + (core + 1 - j % 2) % 2

            @pl.when(to != place)
            def _():
                send(zres.at[c, :, block(y_lo * group + to, cols)], zret_o.at[c, block(place, line_rows)], 4, zret_o_sem.at[c], to_place(to))

            return carry

        lax.fori_loop(first, first + count, step, 0)

    def return_own(c):
        def one(to):
            send(zres.at[c, :, block(y_lo * group + to, cols)], zret_o.at[c, block(place, line_rows)], 4, zret_o_sem.at[c], to_place(to))

        each_place(one)
        zret_o[c, block(place, line_rows)] = zres[c, :, block(wide, cols)]

    def y_part(c):
        if across > 1:
            arrived(yin.at[c, :, pl.ds(0, 2 * (across - 1) * rows)], yin_sem.at[c])
        line_part(yin, yres, 0, 1, c, planes)
        for k in range(1, across):
            to = (x + k) % across
            send(yres.at[c, :, block((1 - y_hi) * across + to, rows)], yret_q.at[c, block(x, planes)], 5, yret_q_sem.at[c], to_x(to))
        for k in range(1, across):
            to = (x + k) % across
            send(yres.at[c, :, block(y_hi * across + to, rows)], yret_p.at[c, block(x, planes)], 5, yret_p_sem.at[c], to_x(to))
        yret_q[c, block(x, planes)] = yres[c, :, block(q_narrow, rows)]
        yret_p[c, block(x, planes)] = yres[c, :, block(narrow, rows)]

    def back_to_q(c):
        if across > 1:
            arrived(yret_q.at[c, pl.ds(0, (across - 1) * planes)], yret_q_sem.at[c])
        send(yret_q.at[c], back_q.at[c], 6, back_q_sem.at[c], q_device)

    def back_to_p(c):
        if across > 1:
            arrived(yret_p.at[c, pl.ds(0, (across - 1) * planes)], yret_p_sem.at[c])
        arrived(zret_p.at[c, pl.ds(0, (group - 1) * line_rows)], zret_p_sem.at[c])
        for plane in range(cols):
            psum[c, :, plane, :] = zret_p[c, :, plane, :] + yret_p[c, plane]
        send(psum.at[c], back_p.at[c], 7, back_p_sem.at[c], p_device)

    def back_to_p_in_halves(c):
        if across > 1:
            arrived(yret_p.at[c, pl.ds(0, (across - 1) * planes)], yret_p_sem.at[c])
        count = deep * line_rows
        for sem, index, senders in ((1, 1 - place // deep, deep), (0, place // deep, deep - 1)):
            arrived(zret_p.at[c, pl.ds(0, senders * line_rows)], half_sem.at[sem])
            part = block(index, count)
            for plane in range(cols):
                psum[c, part, plane, :] = zret_p[c, part, plane, :] + yret_p[c, plane, part, :]
            send(psum.at[c, part], back_p.at[c, part], 7, back_p_sem.at[c], p_device)

    def add_q(c):
        arrived(back_q.at[c], back_q_sem.at[c])
        for plane in range(cols):
            acc[c, :, plane, keep] = acc[c, :, plane, keep] + back_q[c, plane]

    def add_p(c):
        arrived(back_p.at[c], back_p_sem.at[c])
        acc[c, :, :, give] = acc[c, :, :, give] + back_p[c]

    def add_own(c):
        arrived(zret_o.at[c, pl.ds(0, (group - 1) * line_rows)], zret_o_sem.at[c])
        acc[c, :, :, keep] = acc[c, :, :, keep] + zret_o[c]

    send_out(2, 1)
    send_out(1, 2)
    send_out(0, 0)

    load_vel.wait()
    for c in range(3):
        zin[c, :, block(wide, cols)] = velv[c, block(place, line_rows), :, keep]
    for load in loads:
        load.wait()
    for k in range(2):
        hx[k], lx[k] = split((-0.5, 0.5)[k] * opx[k])
    for k in range(4):
        hyz[k], lyz[k] = split((-0.5, 0.5)[k % 2] * opyz[k])

    arrived(pin.at[2], pin_sem.at[2])
    send_z_p(2)
    x_part(2)
    arrived(pin.at[1], pin_sem.at[1])
    send_y(1, pin, ysp, narrow)
    send_z_p(1)
    arrived(qin.at[1], qin_sem.at[1])
    send_y(1, qin, ysq, q_narrow)
    send_y(2, pin, ysp, narrow)
    x_part(1)
    arrived(pin.at[0], pin_sem.at[0])
    send_z_p(0)
    send_y(0, pin, ysp, narrow)
    arrived(qin.at[2], qin_sem.at[2])
    send_y(2, qin, ysq, q_narrow)
    arrived(qin.at[0], qin_sem.at[0])
    send_y(0, qin, ysq, q_narrow)
    x_part(0)

    z_part(2)
    return_own(2)
    y_part(1)
    y_part(2)
    back_to_q(1)
    z_part(1)
    y_part(0)
    back_to_q(2)
    z_part(0)
    return_own(1)
    back_to_q(0)
    back_to_p(2)
    add_q(1)
    add_q(2)
    back_to_p(1)
    add_q(0)
    back_to_p_in_halves(0)
    return_own_low_first(0, 0, group)
    zret_o[0, block(place, line_rows)] = zres[0, :, block(wide, cols)]
    add_p(2)
    add_own(2)
    add_p(1)
    add_own(1)
    add_p(0)
    add_own(0)

    z_blocks = zin.at[:, :, pl.ds(0, 2 * (group - 1) * cols)]
    for k, part in ((0, pin), (1, qin), (2, z_blocks), (4, z_blocks), (6, back_q), (7, back_p)):
        arrived(part, send_sem.at[k])
    if across > 1:
        for k in (3, 5):
            arrived(yin.at[:, :, pl.ds(0, 2 * (across - 1) * rows)], send_sem.at[k])


def on_device(wide_size, narrow_size, *arrays):
    shape = arrays[0].shape
    _, rows, cols, width = shape
    group, across, half = wide_size // 2, narrow_size // 2, width // 2
    z_lines, y_lines = wide_size * cols, narrow_size * rows
    vmem, dma = pltpu.VMEM, pltpu.SemaphoreType.DMA
    part, turned = vmem((3, rows, cols, half), F32), vmem((3, cols, rows, half), F32)
    z_block, y_block = vmem((3, rows // group, z_lines, half), F32), vmem((3, cols // across, y_lines, half), F32)
    return pl.pallas_call(
        functools.partial(kernel, wide_size, narrow_size),
        out_shape=jax.ShapeDtypeStruct(shape, F32),
        in_specs=[pl.BlockSpec(memory_space=pltpu.HBM)] * 7,
        out_specs=pl.BlockSpec(memory_space=pltpu.VMEM),
        scratch_shapes=[
            vmem(shape, F32),
            vmem((2, width, width), F32),
            vmem((4, z_lines, z_lines), F32),
            vmem((2, width, width), BF16),
            vmem((2, width, width), BF16),
            vmem((4, z_lines, z_lines), BF16),
            vmem((4, z_lines, z_lines), BF16),
            part, part, turned, turned, z_block, y_block, z_block, y_block,
            part, part, turned, turned, part, part, turned,
            dma((7,)),
            dma((8,)),
            *[dma((3,))] * 10,
            dma((2,)),
        ],
        compiler_params=pltpu.CompilerParams(
            collective_id=0, has_side_effects=True, vmem_limit_bytes=40 * 1024 * 1024
        ),
    )(*[pltpu.with_memory_space_constraint(array, pltpu.HBM) for array in arrays])


def solution(mesh):
    return jax.shard_map(
        functools.partial(on_device, mesh.shape["wide"], mesh.shape["narrow"]),
        mesh=mesh,
        in_specs=(P(None, "narrow", "wide", None), P(), P(), P(), P(), P(), P()),
        out_specs=P(None, "narrow", "wide", None),
        check_vma=False,
    )
```
